256 devices in a mesh: dp: 8 (over z), expert: 32 (over x, y, core).
Axes of the slice: x: 4, y: 4, z: 8, core: 2. Of those that a mesh axis runs over, the one named last changes fastest.
Arguments:
- grad_out: bfloat16 [32768, 4096], P(('dp', 'expert')), may hold values from -6 to 6
- expert_ids: int32 [32768, 8], P(('dp', 'expert')), may hold values from 0 to 63, all different within a row; in each aligned block of 128 rows (0 to 127, 128 to 255, ...) at most 17 rows name the same one
- gate_weights: bfloat16 [32768, 8], P(('dp', 'expert')), may hold values from 0.019897461 to 0.5
- saved_gate: bfloat16 [64, 4352, 768], P('expert', 'dp'), may hold values from -6 to 6
- saved_up: bfloat16 [64, 4352, 768], P('expert', 'dp'), may hold values from -6 to 6
- down_weight: bfloat16 [768, 64, 4096], P('dp', 'expert'), may hold values from -0.21875 to 0.21875
Outputs:
- grad_gate: bfloat16 [64, 4352, 768], P('expert', 'dp')
- grad_up: bfloat16 [64, 4352, 768], P('expert', 'dp')
- grad_down: float32 [768, 64, 4096], P('dp', 'expert')
The draws below stay inside these ranges and needn't reach their ends.
Inputs may be any that keep to these rules, and one draw needn't show every extreme that they name: `expert_ids`: among the tokens of one device (aligned blocks of 128 rows) no expert is named more than 17 times, a bound that some block reaches; a token names 8 different experts.
All inputs are finite; a program needn't handle non-finite values.
Results may differ from the reference program's by a relative error of at most 0.015.
Values may be sent and summed in bfloat16 or wider, within the bound.
No kernel may reach another device: no remote copies, remote signals or barrier semaphores. Data moves between devices by JAX's collectives and lax.ppermute only.
A program may use at most 192 MiB of HBM per device.

```python
import math
import jax
import jax.numpy as jnp
import numpy as np
from jax import lax

D = 4096
FF = 768
TOP = 8
TOK_DEV = 128
EXPERTS = 64
CAP = 17
SOURCES = 32
GROUPS = 8
TOKENS = 32768
SLOTS = 4352


def levels(stream_key, extent, split, least, high):
    loudness, own = 1.0, jax.random.fold_in(stream_key, 6)
    for axis_at, shards_of in split:
        heights = jnp.exp(jax.random.uniform(jax.random.fold_in(own, axis_at), (shards_of,), jnp.float32, least / len(split), high / len(split)))
        loudness = loudness * jnp.repeat(heights, extent[axis_at] // shards_of).reshape([-1 if axis == axis_at else 1 for axis in range(len(extent))])
    return loudness


def deal_out(key, own, number, rows, count, top, reach, lean):
    sequence = jax.random.permutation(key, count)
    heavy_load, usual = shares(count, rows * top, reach, lean, True), shares(count, rows * top, reach, lean, False)
    places = jnp.arange(count)

    def named(tallies, offset_by):
        used = int((tallies > 0).sum())
        fixed = max(1, used // 4)
        shifted = fixed + (places - fixed + offset_by * (used - fixed)) % max(1, count - fixed)
        return jnp.zeros((count,), jnp.int32).at[sequence[jnp.where(places < fixed, places, shifted)]].set(jnp.asarray(tallies, jnp.int32))

    tallies = jnp.where(number % 4 == 0, named(heavy_load, number // 4), named(usual, number - number // 4 - 1))
    mixed = jax.random.permutation(jax.random.fold_in(own, 3), count)
    source_of, sink = mixed[0:count // 2 * 2:2], mixed[1:count // 2 * 2:2]
    slack = jnp.minimum(tallies[source_of] - 1, reach - tallies[sink]) // 2
    slack = jnp.where((source_of == sequence[0]) | (sink == sequence[0]) | (tallies[sink] == 0), 0, jnp.maximum(slack, 0))
    shifted = jax.random.randint(jax.random.fold_in(own, 4), (count // 2,), 0, 1 << 20) % (slack + 1)
    tallies = tallies.at[source_of].add(-shifted).at[sink].add(shifted)
    labels = jnp.searchsorted(jnp.cumsum(tallies), jnp.arange(rows * top), side="right").astype(jnp.int32)
    listing = labels.reshape(top, rows).T
    listing = listing[jax.random.permutation(jax.random.fold_in(own, 1), rows)]
    offset_by = jax.random.randint(jax.random.fold_in(own, 2), (rows, 1), 0, top)
    return jnp.take_along_axis(listing, (jnp.arange(top)[None, :] + offset_by) % top, axis=1)


def shares(count, total, bound, skew, full):
    portions = [(1 << 20) // math.isqrt(grade ** skew) + 1 for grade in range(1, count + 1)]
    largest = bound if full else min(bound, max(-(-total // count), total * portions[0] // sum(portions)))
    least = 1 if total - largest >= count - 1 else 0
    holding, spare = [largest] + [least] * (count - 1), total - largest - least * (count - 1)
    while spare > 0:
        free = [i for i in range(1, count) if holding[i] < largest] or [i for i in range(1, count) if holding[i] < bound]
        mass, remaining = sum([portions[i] for i in free]), spare
        for i in free:
            extra = min(bound - holding[i], max(1, remaining * portions[i] // mass), spare)
            holding[i] = holding[i] + extra
            spare = spare - extra
    return np.array(holding)


def gaussian(key, shape, deviation, limit, shards=(), kind=jnp.bfloat16):
    array = jax.random.normal(key, shape, jnp.float32) * deviation
    if len(shards) > 0:
        array = levels(key, shape, shards, -0.22, 0.18) * array
    return jnp.clip(array, min=-limit, max=limit).astype(kind)


def setup_inputs(seed: int = 0) -> dict:
    seeds = jax.random.split(jax.random.key(seed), 7)
    grad_out = gaussian(seeds[0], (TOKENS, D), 1.0, 6.0, ((0, 256),))
    expert_ids_keys = jax.random.split(jax.random.fold_in(seeds[1], 1), TOKENS // TOK_DEV)
    expert_ids_turns = jax.random.permutation(jax.random.fold_in(seeds[1], 3), TOKENS // TOK_DEV)
    expert_ids = jax.vmap(lambda own, number: deal_out(jax.random.fold_in(seeds[1], 2), own, number, TOK_DEV, EXPERTS, TOP, CAP, 1))(expert_ids_keys, expert_ids_turns).reshape((TOKENS, TOP))
    gate_weights = jnp.clip(jnp.exp(math.log(0.5) - 3.224016 * jax.random.uniform(seeds[2], (TOKENS, TOP), jnp.float32) ** levels(seeds[2], (TOKENS, TOP), ((0, 256),), -0.2, 0.2)), 0.019897461, 0.5).astype(jnp.bfloat16)
    saved_gate = gaussian(seeds[3], (EXPERTS, SLOTS, FF), 1.0, 6.0, ((0, 32), (1, 8)))
    saved_up = gaussian(seeds[4], (EXPERTS, SLOTS, FF), 1.0, 6.0, ((0, 32), (1, 8)))
    down_weight = gaussian(seeds[5], (FF, EXPERTS, D), FF ** -0.5, 0.21875, ((0, 8), (1, 32)))
    return dict(grad_out=grad_out, expert_ids=expert_ids, gate_weights=gate_weights, saved_gate=saved_gate, saved_up=saved_up, down_weight=down_weight)


def dispatch_group(grad_rows, group_ids, group_gates):
    flat_ids = group_ids.reshape(SOURCES, TOK_DEV * TOP)
    onehot = (flat_ids[:, :, None] == jnp.arange(EXPERTS, dtype=jnp.int32)[None, None, :]).astype(jnp.int32)
    slot_rank = jnp.sum((jnp.cumsum(onehot, axis=1) - onehot) * onehot, axis=2).astype(jnp.int32)
    weighted = group_gates.reshape(SOURCES, TOK_DEV, TOP, 1).astype(jnp.float32) * grad_rows.reshape(SOURCES, TOK_DEV, 1, D).astype(jnp.float32)
    weighted = weighted.reshape(SOURCES, TOK_DEV * TOP, D).astype(jnp.bfloat16)
    source_idx = jnp.broadcast_to(jnp.arange(SOURCES, dtype=jnp.int32)[:, None], (SOURCES, TOK_DEV * TOP))
    buffer = jnp.zeros((EXPERTS, SOURCES, CAP, D), jnp.bfloat16)
    buffer = buffer.at[flat_ids, source_idx, slot_rank].set(weighted)
    return buffer.reshape(EXPERTS, SOURCES * CAP, D)


def expert_backward(operands):
    rows, gate, up, weight = operands
    gate_f = gate.astype(jnp.float32)
    up_f = up.astype(jnp.float32)
    logistic = jax.nn.sigmoid(gate_f)
    activated = gate_f * logistic
    hidden = (activated * up_f).astype(jnp.bfloat16)
    grad_hidden = jnp.dot(rows, weight.T, preferred_element_type=jnp.float32)
    grad_gate = (grad_hidden * up_f * logistic * (1.0 + gate_f * (1.0 - logistic))).astype(jnp.bfloat16)
    grad_up = (grad_hidden * activated).astype(jnp.bfloat16)
    partial_value = jnp.dot(hidden.T, rows, preferred_element_type=jnp.float32).astype(jnp.bfloat16)
    return grad_gate, grad_up, partial_value


def reference(grad_out, expert_ids, gate_weights, saved_gate, saved_up, down_weight):
    group_rows = SOURCES * CAP
    group_tokens = SOURCES * TOK_DEV
    gate_all = saved_gate.reshape(EXPERTS, GROUPS, group_rows, FF)
    up_all = saved_up.reshape(EXPERTS, GROUPS, group_rows, FF)
    weights = jnp.transpose(down_weight, (1, 0, 2))

    def one_group(total, group):
        start = (group * group_tokens).astype(jnp.int32)
        grad_rows = lax.dynamic_slice_in_dim(grad_out, start, group_tokens, 0)
        group_ids = lax.dynamic_slice_in_dim(expert_ids, start, group_tokens, 0)
        group_gates = lax.dynamic_slice_in_dim(gate_weights, start, group_tokens, 0)
        dispatched = dispatch_group(grad_rows, group_ids, group_gates)
        gate_here = lax.dynamic_index_in_dim(gate_all, group, 1, keepdims=False)
        up_here = lax.dynamic_index_in_dim(up_all, group, 1, keepdims=False)
        grad_gate, grad_up, partial_value = lax.map(expert_backward, (dispatched, gate_here, up_here, weights))
        return total + partial_value.astype(jnp.float32), (grad_gate, grad_up)

    initial = jnp.zeros((EXPERTS, FF, D), jnp.float32)
    total, (grad_gate, grad_up) = lax.scan(one_group, initial, jnp.arange(GROUPS, dtype=jnp.int32))
    grad_gate = jnp.transpose(grad_gate, (1, 0, 2, 3)).reshape(EXPERTS, GROUPS * group_rows, FF)
    grad_up = jnp.transpose(grad_up, (1, 0, 2, 3)).reshape(EXPERTS, GROUPS * group_rows, FF)
    grad_down = jnp.transpose(total, (1, 0, 2))
    return grad_gate, grad_up, grad_down
```

```python
import functools

import jax
import jax.numpy as jnp
from jax import lax
from jax.experimental import pallas as pl
from jax.experimental.pallas import tpu as pltpu
from jax.sharding import PartitionSpec as P

BF = jnp.bfloat16
F32 = jnp.float32
LANE = 128
MAIN = 16
FOLD = 8
PARAMS = pltpu.CompilerParams(vmem_limit_bytes=56 * 1024 * 1024)


def dot(a, b, dims=((1,), (0,))):
    return lax.dot_general(a, b, (dims, ((), ())), preferred_element_type=F32)


def iota(shape, dim):
    return lax.broadcasted_iota(jnp.int32, shape, dim)


def dispatch_kernel(ids_ref, gates_ref, grad_ref, out_ref, main_ref, tail_ref):
    step = pl.program_id(0)
    tokens, top = ids_ref.shape
    dests = out_ref.shape[0]
    experts = 2 * dests

    @pl.when(step == 0)
    def _():
        lanes = iota((tokens, LANE), 1)
        member = jnp.zeros((tokens, LANE), F32)
        gate = jnp.zeros((tokens, LANE), F32)
        for k in range(top):
            hit = ids_ref[:, k : k + 1] == lanes
            member = member + jnp.where(hit, 1.0, 0.0)
            gate = gate + jnp.where(hit, gates_ref[:, k : k + 1].astype(F32), 0.0)
        earlier = jnp.where(iota((tokens, tokens), 1) < iota((tokens, tokens), 0), 1.0, 0.0)
        rank = dot(earlier.astype(BF), member.astype(BF))
        rank = jnp.where(member > 0.0, rank, -1.0)
        rank_t = jnp.transpose(rank)[:experts]
        gate_t = jnp.transpose(gate)[:experts]
        slots = iota((experts, MAIN, tokens), 1).astype(F32)
        chosen = jnp.where(rank_t[:, None, :] == slots, gate_t[:, None, :], 0.0)
        main_ref[...] = chosen.reshape(experts * MAIN, tokens).astype(BF)
        last = jnp.where(rank_t == float(MAIN), gate_t, 0.0)
        last = jnp.broadcast_to(last[:, None, :], (experts, FOLD, tokens)).reshape(experts * FOLD, tokens)
        rows = iota((experts * FOLD, tokens), 0) % FOLD
        for k in range(FOLD):
            tail_ref[:, k * tokens : (k + 1) * tokens] = jnp.where(rows == k, last, 0.0).astype(BF)

    @pl.when(step < pl.num_programs(0) - 1)
    def _():
        columns = grad_ref[:, pl.ds(pl.multiple_of(step * 256, 256), 256)]
        rows = dot(main_ref[...], columns).astype(BF)
        for k in range(2):
            out_ref[:, k * 32 : (k + 1) * 32, :] = rows[:, k * LANE : (k + 1) * LANE].reshape(dests, 32, LANE)

    @pl.when(step == pl.num_programs(0) - 1)
    def _():
        width = grad_ref.shape[1] // FOLD
        stacked = jnp.concatenate([grad_ref[:, k * width : (k + 1) * width] for k in range(FOLD)], axis=0)
        rows = dot(tail_ref[...], stacked).astype(BF)
        for k in range(width // LANE):
            out_ref[:, k * 16 : (k + 1) * 16, :] = rows[:, k * LANE : (k + 1) * LANE].reshape(dests, 16, LANE)


def dispatch(ids, gates, grad, dests):
    tokens, width = grad.shape
    rows = 34 * width // LANE
    steps = rows // 64
    return pl.pallas_call(
        dispatch_kernel,
        grid=(steps,),
        in_specs=[
            pl.BlockSpec(ids.shape, lambda i: (0, 0)),
            pl.BlockSpec(gates.shape, lambda i: (0, 0)),
            pl.BlockSpec(grad.shape, lambda i: (0, 0)),
        ],
        out_specs=pl.BlockSpec((dests, 64, LANE), lambda i: (0, i, 0)),
        out_shape=jax.ShapeDtypeStruct((dests, rows, LANE), BF),
        scratch_shapes=[
            pltpu.VMEM((2 * dests * MAIN, tokens), BF),
            pltpu.VMEM((2 * dests * FOLD, FOLD * tokens), BF),
        ],
        compiler_params=PARAMS,
        cost_estimate=pl.CostEstimate(flops=2 * 1088 * 128 * 4096, bytes_accessed=10 << 20, transcendentals=0),
        name="dispatch",
    )(ids, gates, grad)


def natural(order, sources):
    main = sources * MAIN
    return jnp.where(order < main, (order // MAIN) * (MAIN + 1) + order % MAIN, (order - main) * (MAIN + 1) + MAIN)


def hidden_kernel(sources, gate_ref, up_ref, out_ref):
    gate = gate_ref[0].astype(F32)
    slots = gate.shape[0]
    hidden = (gate * jax.nn.sigmoid(gate) * up_ref[0].astype(F32)).astype(BF)
    place = natural(iota((slots, slots), 1), sources) == iota((slots, slots), 0)
    place = jnp.where(place, 1.0, 0.0).astype(BF)
    out_ref[0] = dot(hidden, place, ((0,), (0,))).astype(BF)


def arranged_hidden(gate, up, sources):
    local, slots, units = gate.shape
    spec = pl.BlockSpec((1, slots, units), lambda e: (e, 0, 0))
    return pl.pallas_call(
        functools.partial(hidden_kernel, sources),
        grid=(local,),
        in_specs=[spec, spec],
        out_specs=pl.BlockSpec((1, units, slots), lambda e: (e, 0, 0)),
        out_shape=jax.ShapeDtypeStruct((local, units, slots), BF),
        compiler_params=PARAMS,
        cost_estimate=pl.CostEstimate(flops=4 * slots * slots * units, bytes_accessed=6 << 20, transcendentals=local * slots * units),
        name="hidden",
    )(gate, up)


def unfold(tail_ref, out_ref):
    sources = tail_ref.shape[0]
    rows = sources * 16
    folded = jnp.concatenate([tail_ref[:, k * 16 : (k + 1) * 16, :].reshape(rows, LANE) for k in range(4)], axis=1)
    row = iota((2 * sources, rows), 0)
    column = iota((2 * sources, rows), 1)
    for k in range(FOLD):
        pick = column == (row % sources) * 16 + (row // sources) * FOLD + k
        out_ref[k] = dot(jnp.where(pick, 1.0, 0.0).astype(BF), folded).astype(BF)


def expert_rows(rows_ref, expert):
    sources = rows_ref.shape[0]
    return jnp.concatenate(
        [
            rows_ref[:, k * 32 + expert * 16 : k * 32 + expert * 16 + 16, :].reshape(sources * 16, LANE)
            for k in range(4)
        ],
        axis=1,
    )


def down_kernel(rows_ref, tail_ref, hidden_ref, out_ref, last_ref):
    step = pl.program_id(0)
    sources = rows_ref.shape[0]

    @pl.when(step == 0)
    def _():
        unfold(tail_ref, last_ref)

    groups, _, units, width = out_ref.shape
    main = sources * MAIN
    for e in range(2):
        total = dot(hidden_ref[e][:, :main], expert_rows(rows_ref, e))
        total = total + dot(hidden_ref[e][:, main:], last_ref[step, e * sources : (e + 1) * sources, :])
        out_ref[:, e] = total.astype(BF).reshape(groups, units, width)


def partial_down(arrived, hidden, groups):
    sources, rows, _ = arrived.shape
    _, units, slots = hidden.shape
    width = rows // 34 * LANE
    return pl.pallas_call(
        down_kernel,
        grid=(FOLD,),
        in_specs=[
            pl.BlockSpec((sources, 128, LANE), lambda i: (0, i, 0)),
            pl.BlockSpec((sources, 64, LANE), lambda i: (0, 16, 0)),
            pl.BlockSpec(hidden.shape, lambda i: (0, 0, 0)),
        ],
        out_specs=pl.BlockSpec((groups, 2, units // groups, 512), lambda i: (0, 0, 0, i)),
        out_shape=jax.ShapeDtypeStruct((groups, 2, units // groups, width), BF),
        scratch_shapes=[pltpu.VMEM((FOLD, 2 * sources, 512), BF)],
        compiler_params=PARAMS,
        cost_estimate=pl.CostEstimate(flops=4 * slots * units * width, bytes_accessed=24 << 20, transcendentals=0),
        name="partial_down",
    )(arrived, arrived, hidden)


def gate_kernel(rows_ref, tail_ref, weight_ref, gate_ref, up_ref, grad_gate_ref, grad_up_ref, last_ref, total_ref):
    step = pl.program_id(0)
    sources = rows_ref.shape[0]
    main = sources * MAIN
    slots = gate_ref.shape[1]

    @pl.when(step == 0)
    def _():
        unfold(tail_ref, last_ref)
        total_ref[...] = jnp.zeros_like(total_ref)

    groups, _, units, width = weight_ref.shape
    for e in range(2):
        weight = weight_ref[:, e].reshape(groups * units, width)
        total_ref[e, :main] += dot(expert_rows(rows_ref, e), weight, ((1,), (1,)))
        total_ref[e, main:] += dot(last_ref[step, e * sources : (e + 1) * sources, :], weight, ((1,), (1,)))

    @pl.when(step == pl.num_programs(0) - 1)
    def _():
        place = natural(iota((slots, slots), 0), sources) == iota((slots, slots), 1)
        place = jnp.where(place, 1.0, 0.0).astype(BF)
        back = natural(iota((slots, slots), 1), sources) == iota((slots, slots), 0)
        back = jnp.where(back, 1.0, 0.0).astype(BF)
        for e in range(2):
            gate = dot(place, gate_ref[e])
            up = dot(place, up_ref[e])
            logistic = jax.nn.sigmoid(gate)
            grad = total_ref[e]
            grad_gate = (grad * up * logistic * (1.0 + gate * (1.0 - logistic))).astype(BF)
            grad_up = (grad * (gate * logistic)).astype(BF)
            grad_gate_ref[e] = dot(back, grad_gate).astype(BF)
            grad_up_ref[e] = dot(back, grad_up).astype(BF)


def gate_grads(arrived, weights, gate, up):
    sources, rows, _ = arrived.shape
    groups, _, units, width = weights.shape
    _, slots, all_units = gate.shape
    whole = pl.BlockSpec(gate.shape, lambda i: (0, 0, 0))
    return pl.pallas_call(
        gate_kernel,
        grid=(FOLD,),
        in_specs=[
            pl.BlockSpec((sources, 128, LANE), lambda i: (0, i, 0)),
            pl.BlockSpec((sources, 64, LANE), lambda i: (0, 16, 0)),
            pl.BlockSpec((groups, 2, units, 512), lambda i: (0, 0, 0, i)),
            whole,
            whole,
        ],
        out_specs=[whole, whole],
        out_shape=[jax.ShapeDtypeStruct(gate.shape, BF)] * 2,
        scratch_shapes=[
            pltpu.VMEM((FOLD, 2 * sources, 512), BF),
            pltpu.VMEM((2, slots, all_units), F32),
        ],
        compiler_params=PARAMS,
        cost_estimate=pl.CostEstimate(flops=4 * slots * all_units * width, bytes_accessed=32 << 20, transcendentals=2 * slots * all_units),
        name="gate_grads",
    )(arrived, arrived, weights, gate, up)


def on_device(grad_out, expert_ids, gate_weights, saved_gate, saved_up, down_weight):
    sources = lax.axis_size("expert")
    groups = lax.axis_size("dp")
    units, local, width = down_weight.shape
    weights = lax.all_gather(jnp.transpose(down_weight, (1, 0, 2)), "dp", axis=0, tiled=False)
    rows = dispatch(expert_ids, gate_weights, grad_out, sources)
    arrived = lax.all_to_all(rows, "expert", split_axis=0, concat_axis=0, tiled=True)
    hidden = arranged_hidden(saved_gate, saved_up, sources)
    partial = partial_down(arrived, hidden, groups)
    summed = lax.psum_scatter(
        partial.reshape(groups, local * units, width), "dp", scatter_dimension=0, tiled=True
    )
    grad_gate, grad_up = gate_grads(arrived, weights, saved_gate, saved_up)
    grad_down = jnp.transpose(summed.reshape(local, units, width), (1, 0, 2)).astype(F32)
    return (grad_gate, grad_up, grad_down)


def solution(mesh):
    in_specs = (
        P(("dp", "expert"), None),
        P(("dp", "expert"), None),
        P(("dp", "expert"), None),
        P("expert", "dp", None),
        P("expert", "dp", None),
        P("dp", "expert", None),
    )
    out_specs = (P("expert", "dp", None), P("expert", "dp", None), P("dp", "expert", None))
    return jax.shard_map(
        on_device, mesh=mesh, in_specs=in_specs, out_specs=out_specs, check_vma=False
    )
```

```python
import functools

import jax
import jax.numpy as jnp
from jax import lax
from jax.experimental import pallas as pl
from jax.experimental.pallas import tpu as pltpu
from jax.sharding import PartitionSpec as P

BF = jnp.bfloat16
F32 = jnp.float32
LANE = 128
MAIN = 16
FOLD = 8
WIDE = FOLD * LANE
BLOCK = 2 * MAIN * FOLD + 2 * FOLD
PARAMS = pltpu.CompilerParams(vmem_limit_bytes=56 * 1024 * 1024)


def dot(a, b, dims=((1,), (0,))):
    return lax.dot_general(a, b, (dims, ((), ())), preferred_element_type=F32)


def iota(shape, dim):
    return lax.broadcasted_iota(jnp.int32, shape, dim)


def dispatch_kernel(ids_ref, gates_ref, grad_ref, out_ref, main_ref, tail_ref):
    top, tokens = ids_ref.shape
    dests = out_ref.shape[0]
    experts = 2 * dests

    @pl.when(pl.program_id(0) == 0)
    def _():
        expert = iota((experts, tokens), 0)
        member = jnp.zeros((experts, tokens), F32)
        gate = jnp.zeros((experts, tokens), F32)
        gates = gates_ref[...].astype(F32)
        for k in range(top):
            hit = ids_ref[k : k + 1, :] == expert
            member = jnp.where(hit, 1.0, member)
            gate = jnp.where(hit, gates[k : k + 1, :], gate)
        earlier = jnp.where(iota((tokens, tokens), 0) < iota((tokens, tokens), 1), 1.0, 0.0)
        rank = dot(member.astype(BF), earlier.astype(BF))
        rank = jnp.where(member > 0.0, rank, -1.0)
        slots = iota((experts, MAIN, tokens), 1).astype(F32)
        chosen = jnp.where(rank[:, None, :] == slots, gate[:, None, :], 0.0)
        main_ref[...] = chosen.reshape(experts * MAIN, tokens).astype(BF)
        last = jnp.where(rank == float(MAIN), gate, 0.0)
        last = jnp.broadcast_to(last[:, None, :], (experts, FOLD, tokens)).reshape(experts * FOLD, tokens)
        rows = iota((experts * FOLD, tokens), 0) % FOLD
        for k in range(FOLD):
            tail_ref[:, k * tokens : (k + 1) * tokens] = jnp.where(rows == k, last, 0.0).astype(BF)

    for pair in range(FOLD // 2):
        rows = dot(main_ref[...], grad_ref[:, pair * 256 : (pair + 1) * 256]).astype(BF)
        for k in range(2):
            at = (2 * pair + k) * 2 * MAIN
            out_ref[:, at : at + 2 * MAIN, :] = rows[:, k * LANE : (k + 1) * LANE].reshape(dests, 2 * MAIN, LANE)
    stacked = jnp.concatenate([grad_ref[:, k * LANE : (k + 1) * LANE] for k in range(FOLD)], axis=0)
    rows = dot(tail_ref[...], stacked).astype(BF)
    out_ref[:, 2 * MAIN * FOLD :, :] = rows.reshape(dests, 2 * FOLD, LANE)


def dispatch(ids, gates, grad, dests, first, count):
    tokens, _ = grad.shape
    ids, gates = jnp.transpose(ids), jnp.transpose(gates)
    return pl.pallas_call(
        dispatch_kernel,
        grid=(count,),
        in_specs=[
            pl.BlockSpec(ids.shape, lambda i: (0, 0)),
            pl.BlockSpec(gates.shape, lambda i: (0, 0)),
            pl.BlockSpec((tokens, WIDE), lambda i: (0, first + i)),
        ],
        out_specs=pl.BlockSpec((dests, BLOCK, LANE), lambda i: (0, i, 0)),
        out_shape=jax.ShapeDtypeStruct((dests, count * BLOCK, LANE), BF),
        scratch_shapes=[
            pltpu.VMEM((2 * dests * MAIN, tokens), BF),
            pltpu.VMEM((2 * dests * FOLD, FOLD * tokens), BF),
        ],
        compiler_params=PARAMS,
        cost_estimate=pl.CostEstimate(
            flops=count * 2 * 1088 * 128 * WIDE, bytes_accessed=count * 3 << 20, transcendentals=0
        ),
        name="dispatch",
    )(ids, gates, grad)


def natural(order, sources):
    main = sources * MAIN
    return jnp.where(order < main, (order // MAIN) * (MAIN + 1) + order % MAIN, (order - main) * (MAIN + 1) + MAIN)


def arrange_kernel(sources, gate_ref, up_ref, hidden_ref, gate_out_ref, up_out_ref):
    gate = gate_ref[0].astype(F32)
    slots = gate.shape[0]
    hidden = (gate * jax.nn.sigmoid(gate) * up_ref[0].astype(F32)).astype(BF)
    place = natural(iota((slots, slots), 1), sources) == iota((slots, slots), 0)
    place = jnp.where(place, 1.0, 0.0).astype(BF)
    hidden_ref[0] = dot(hidden, place, ((0,), (0,))).astype(BF)
    place = natural(iota((slots, slots), 0), sources) == iota((slots, slots), 1)
    place = jnp.where(place, 1.0, 0.0).astype(BF)
    gate_out_ref[0] = dot(place, gate_ref[0]).astype(BF)
    up_out_ref[0] = dot(place, up_ref[0]).astype(BF)


def arrange(gate, up, sources):
    local, slots, units = gate.shape
    spec = pl.BlockSpec((1, slots, units), lambda e: (e, 0, 0))
    return pl.pallas_call(
        functools.partial(arrange_kernel, sources),
        grid=(local,),
        in_specs=[spec, spec],
        out_specs=[pl.BlockSpec((1, units, slots), lambda e: (e, 0, 0)), spec, spec],
        out_shape=[jax.ShapeDtypeStruct((local, units, slots), BF)] + [jax.ShapeDtypeStruct(gate.shape, BF)] * 2,
        compiler_params=PARAMS,
        cost_estimate=pl.CostEstimate(flops=12 * slots * slots * units, bytes_accessed=9 << 20, transcendentals=0),
        name="arrange",
    )(gate, up)


def expert_rows(rows_ref, expert, out_ref):
    sources = rows_ref.shape[0]
    main = sources * MAIN
    for k in range(FOLD):
        at = (2 * k + expert) * MAIN
        out_ref[:main, k * LANE : (k + 1) * LANE] = rows_ref[:, at : at + MAIN, :].reshape(main, LANE)
    at = 2 * MAIN * FOLD
    folded = rows_ref[:, at : at + 2 * FOLD, :].reshape(sources * 2 * FOLD, LANE)
    row = iota((FOLD * sources, sources * 2 * FOLD), 0)
    column = iota((FOLD * sources, sources * 2 * FOLD), 1)
    pick = column == (row % sources) * 2 * FOLD + expert * FOLD + row // sources
    last = dot(jnp.where(pick, 1.0, 0.0).astype(BF), folded).astype(BF)
    for k in range(FOLD):
        out_ref[main:, k * LANE : (k + 1) * LANE] = last[k * sources : (k + 1) * sources]


def down_kernel(place_ref, rows_ref, hidden_ref, slots_ref, rest_ref, first_ref):
    e = pl.program_id(1)
    groups = rest_ref.shape[0]
    units = hidden_ref.shape[1] // groups
    for local in range(2):

        @pl.when(e == local)
        def _():
            expert_rows(rows_ref, local, slots_ref.at[0])

    for n in range(WIDE // 256):
        columns = slice(n * 256, (n + 1) * 256)
        total = dot(hidden_ref[0], slots_ref[0, :, columns]).astype(BF)
        for c in range(groups):
            turn = lax.rem(place_ref[1] * (place_ref[0] - c) - 1 + 2 * groups, groups)
            rest_ref[turn, :, columns] = total[c * units : (c + 1) * units]
    first_ref[...] = rest_ref[0]


def partial_down(place, arrived, hidden, groups, at, count):
    sources, _, _ = arrived.shape
    _, units, slots = hidden.shape
    rows = units // groups
    return pl.pallas_call(
        down_kernel,
        grid=(count, 2),
        in_specs=[
            pl.BlockSpec(memory_space=pltpu.SMEM),
            pl.BlockSpec((sources, BLOCK, LANE), lambda q, e: (0, at + q, 0)),
            pl.BlockSpec((1, units, slots), lambda q, e: (e, 0, 0)),
        ],
        out_specs=[
            pl.BlockSpec((1, slots, WIDE), lambda q, e: (e, 0, q)),
            pl.BlockSpec((groups, rows, WIDE), lambda q, e: (0, e, q)),
            pl.BlockSpec((rows, WIDE), lambda q, e: (e, q)),
        ],
        out_shape=[
            jax.ShapeDtypeStruct((2, slots, count * WIDE), BF),
            jax.ShapeDtypeStruct((groups, 2 * rows, count * WIDE), BF),
            jax.ShapeDtypeStruct((2 * rows, count * WIDE), BF),
        ],
        compiler_params=PARAMS,
        cost_estimate=pl.CostEstimate(
            flops=count * 4 * slots * units * WIDE, bytes_accessed=count * 9 << 20, transcendentals=0
        ),
        name="partial_down",
    )(place, arrived, hidden)


def hidden_grad_kernel(count, *refs):
    weight_ref, total_ref = refs[-2:]
    step = pl.program_id(0)
    groups, _, units, width = weight_ref.shape
    steps = 2 * WIDE // width
    slots_refs = refs[1 : 1 + count]

    @pl.when(step == 0)
    def _():
        total_ref[...] = refs[-3][...] if len(refs) == count + 4 else jnp.zeros_like(total_ref)

    for k, slots_ref in enumerate(slots_refs):

        @pl.when(step // (steps // count) == k)
        def _():
            weight = weight_ref[:, 0].reshape(groups * units, width)
            for n in range(0, groups * units, 256):
                total_ref[:, n : n + 256] += dot(slots_ref[0], weight[n : n + 256], ((1,), (1,)))


def hidden_grad(after, rows, weights, half, expert, before=()):
    groups, _, units, _ = weights.shape
    slots = rows[0].shape[1]
    width = WIDE // 2
    count = len(rows)
    each = 2 * WIDE // width // count
    whole = pl.BlockSpec((slots, groups * units), lambda k: (0, 0))
    specs = [
        pl.BlockSpec((1, slots, width), lambda k, j=j: (expert, 0, jnp.clip(k - j * each, 0, each - 1)))
        for j in range(count)
    ]
    return pl.pallas_call(
        functools.partial(hidden_grad_kernel, count),
        grid=(each * count,),
        in_specs=[pl.BlockSpec(memory_space=pltpu.SMEM)]
        + specs
        + [whole] * len(before)
        + [pl.BlockSpec((groups, 1, units, width), lambda k: (0, expert, 0, half * each * count + k))],
        out_specs=whole,
        out_shape=jax.ShapeDtypeStruct((slots, groups * units), F32),
        compiler_params=PARAMS,
        cost_estimate=pl.CostEstimate(
            flops=4 * slots * groups * units * WIDE, bytes_accessed=9 << 20, transcendentals=0
        ),
        name="hidden_grad",
    )(after, *rows, *before, weights)


def gate_grads_kernel(sources, after_ref, total_ref, gate_ref, up_ref, *refs):
    grad_gate_ref, grad_up_ref = refs[-2:]
    slots, _ = total_ref.shape
    back = natural(iota((slots, slots), 1), sources) == iota((slots, slots), 0)
    back = jnp.where(back, 1.0, 0.0).astype(BF)
    gate = gate_ref[0].astype(F32)
    up = up_ref[0].astype(F32)
    logistic = jax.nn.sigmoid(gate)
    grad = total_ref[...]
    grad_gate = (grad * up * logistic * (1.0 + gate * (1.0 - logistic))).astype(BF)
    grad_up = (grad * (gate * logistic)).astype(BF)
    grad_gate_ref[0] = dot(back, grad_gate).astype(BF)
    grad_up_ref[0] = dot(back, grad_up).astype(BF)


def gate_grads(after, total, gate, up, sources, expert, done=()):
    one = pl.BlockSpec((1,) + gate.shape[1:], lambda i: (expert, 0, 0))
    return pl.pallas_call(
        functools.partial(gate_grads_kernel, sources),
        grid=(1,),
        in_specs=[
            pl.BlockSpec(memory_space=pltpu.SMEM),
            pl.BlockSpec(total.shape, lambda i: (0, 0)),
            one,
            one,
        ]
        + [pl.BlockSpec(memory_space=pl.ANY)] * len(done),
        out_specs=[one, one],
        out_shape=[jax.ShapeDtypeStruct(gate.shape, BF)] * 2,
        input_output_aliases={4 + k: k for k in range(len(done))},
        compiler_params=PARAMS,
        cost_estimate=pl.CostEstimate(flops=4 * 544 * 544 * 768, bytes_accessed=5 << 20, transcendentals=0),
        name="gate_grads",
    )(after, total, gate, up, *done)


def final_kernel(after_ref, own_ref, arrived_ref, *refs):
    out_ref = refs[-1]
    units, _, _ = out_ref.shape
    value = arrived_ref[...].astype(F32) + own_ref[0].astype(F32)
    for e in range(2):
        out_ref[:, e, :] = value[e * units : (e + 1) * units]


def final(after, arrived, rest, shape, at, done=()):
    groups, rows, width = rest.shape
    return pl.pallas_call(
        final_kernel,
        grid=(width // WIDE,),
        in_specs=[
            pl.BlockSpec(memory_space=pltpu.SMEM),
            pl.BlockSpec((1, rows, WIDE), lambda i: (groups - 1, 0, i)),
            pl.BlockSpec((rows, WIDE), lambda i: (0, i)),
        ]
        + [pl.BlockSpec(memory_space=pl.ANY)] * len(done),
        out_specs=pl.BlockSpec((shape[0], 2, WIDE), lambda i: (0, 0, at + i)),
        out_shape=jax.ShapeDtypeStruct(shape, F32),
        input_output_aliases={3 + k: k for k in range(len(done))},
        compiler_params=PARAMS,
        cost_estimate=pl.CostEstimate(flops=rows * width, bytes_accessed=3 << 20, transcendentals=0),
        name="final",
    )(after, rest, arrived, *done)


class Clock:
    def __init__(self, value):
        self.value = value

    def __call__(self, value):
        value, self.value = lax.optimization_barrier((value, self.value))
        return value


class Ring:
    def __init__(self, clock, rest, blocks):
        self.clock, self.rest, self.turn = clock, rest, 0
        groups, members = lax.axis_size("dp"), lax.axis_size("expert")
        self.pairs = [
            (g * members + j, (g + 1 - 2 * (j % 2)) % groups * members + j)
            for g in range(groups)
            for j in range(members)
        ]
        self.send(blocks)

    def send(self, blocks):
        self.got = lax.ppermute(blocks, ("dp", "expert"), self.pairs)

    def step(self):
        self.turn += 1
        self.send(self.clock(self.clock(self.got) + self.rest[self.turn]))


def on_device(grad_out, expert_ids, gate_weights, saved_gate, saved_up, down_weight):
    sources = lax.axis_size("expert")
    groups = lax.axis_size("dp")
    units, local, width = down_weight.shape
    place = jnp.stack([lax.axis_index("dp"), 1 - 2 * (lax.axis_index("expert") % 2)]).astype(jnp.int32)
    clock = Clock(place)

    def exchange(rows):
        return lax.all_to_all(rows, "expert", split_axis=0, concat_axis=0, tiled=True)

    weights = lax.all_gather(jnp.transpose(down_weight, (1, 0, 2)), "dp", axis=0, tiled=False)
    arrived = [exchange(dispatch(expert_ids, gate_weights, grad_out, sources, at, 2)) for at in (0, 2)]
    hidden, gate, up = arrange(saved_gate, saved_up, sources)

    slots, rings, total = [], [], [(), ()]
    for half in range(2):
        rows, rest, sent = partial_down(place, clock(arrived[half]), hidden, groups, 0, 2)
        slots.append(rows)
        rings.append(Ring(clock, rest, clock(sent)))

    def hidden_piece(half, e):
        piece = hidden_grad(clock.value, [slots[half]], weights, half, e, total[e])
        total[e] = (clock(piece),)

    def gate_piece(e, done):
        return clock(gate_grads(clock.value, total[e][0], gate, up, sources, e, done))

    grads = ()
    for turn in range(1, groups - 1):
        rings[0].step()
        if turn in (1, 2, 4, 5):
            hidden_piece((turn - 1) % 3, turn // 3)
        else:
            grads = gate_piece(turn // 3 - 1, grads)
        rings[1].step()
    out_shape, grad_down = (units, local, width), ()
    for half in range(2):
        got = clock(rings[half].got)
        grad_down = (final(clock.value, got, rings[half].rest, out_shape, 2 * half, grad_down),)
    return (grads[0], grads[1], grad_down[0])


def solution(mesh):
    in_specs = (
        P(("dp", "expert"), None),
        P(("dp", "expert"), None),
        P(("dp", "expert"), None),
        P("expert", "dp", None),
        P("expert", "dp", None),
        P("dp", "expert", None),
    )
    out_specs = (P("expert", "dp", None), P("expert", "dp", None), P("dp", "expert", None))
    return jax.shard_map(
        on_device, mesh=mesh, in_specs=in_specs, out_specs=out_specs, check_vma=False
    )
```

```python
import functools

import jax
import jax.numpy as jnp
from jax import lax
from jax.experimental import pallas as pl
from jax.experimental.pallas import tpu as pltpu
from jax.sharding import PartitionSpec as P

BF = jnp.bfloat16
F32 = jnp.float32
LANE = 128
MAIN = 16
FOLD = 8
WIDE = FOLD * LANE
BLOCK = 2 * MAIN * FOLD + 2 * FOLD
PARAMS = pltpu.CompilerParams(vmem_limit_bytes=56 * 1024 * 1024)


def dot(a, b, dims=((1,), (0,))):
    return lax.dot_general(a, b, (dims, ((), ())), preferred_element_type=F32)


def iota(shape, dim):
    return lax.broadcasted_iota(jnp.int32, shape, dim)


def dispatch_kernel(ids_ref, gates_ref, grad_ref, *refs):
    out_ref, main_ref, tail_ref = refs[-3:]
    top, tokens = ids_ref.shape
    dests = out_ref.shape[0]
    experts = 2 * dests

    @pl.when(pl.program_id(0) == 0)
    def _():
        expert = iota((experts, tokens), 0)
        member = jnp.zeros((experts, tokens), F32)
        gate = jnp.zeros((experts, tokens), F32)
        gates = gates_ref[...].astype(F32)
        for k in range(top):
            hit = ids_ref[k : k + 1, :] == expert
            member = jnp.where(hit, 1.0, member)
            gate = jnp.where(hit, gates[k : k + 1, :], gate)
        earlier = jnp.where(iota((tokens, tokens), 0) < iota((tokens, tokens), 1), 1.0, 0.0)
        rank = dot(member.astype(BF), earlier.astype(BF))
        rank = jnp.where(member > 0.0, rank, -1.0)
        slots = iota((experts, MAIN, tokens), 1).astype(F32)
        chosen = jnp.where(rank[:, None, :] == slots, gate[:, None, :], 0.0)
        main_ref[...] = chosen.reshape(experts * MAIN, tokens).astype(BF)
        last = jnp.where(rank == float(MAIN), gate, 0.0)
        last = jnp.broadcast_to(last[:, None, :], (experts, FOLD, tokens)).reshape(experts * FOLD, tokens)
        rows = iota((experts * FOLD, tokens), 0) % FOLD
        for k in range(FOLD):
            tail_ref[:, k * tokens : (k + 1) * tokens] = jnp.where(rows == k, last, 0.0).astype(BF)

    for pair in range(FOLD // 2):
        rows = dot(main_ref[...], grad_ref[:, pair * 256 : (pair + 1) * 256]).astype(BF)
        for k in range(2):
            at = (2 * pair + k) * 2 * MAIN
            out_ref[:, at : at + 2 * MAIN, :] = rows[:, k * LANE : (k + 1) * LANE].reshape(dests, 2 * MAIN, LANE)
    stacked = jnp.concatenate([grad_ref[:, k * LANE : (k + 1) * LANE] for k in range(FOLD)], axis=0)
    rows = dot(tail_ref[...], stacked).astype(BF)
    out_ref[:, 2 * MAIN * FOLD :, :] = rows.reshape(dests, 2 * FOLD, LANE)


def dispatch(ids, gates, grad, dests, first, count, after=()):
    tokens, _ = grad.shape
    ids, gates = jnp.transpose(ids), jnp.transpose(gates)
    return pl.pallas_call(
        dispatch_kernel,
        grid=(count,),
        in_specs=[
            pl.BlockSpec(ids.shape, lambda i: (0, 0)),
            pl.BlockSpec(gates.shape, lambda i: (0, 0)),
            pl.BlockSpec((tokens, WIDE), lambda i: (0, first + i)),
        ]
        + [pl.BlockSpec(memory_space=pl.ANY)] * len(after),
        out_specs=pl.BlockSpec((dests, BLOCK, LANE), lambda i: (0, i, 0)),
        out_shape=jax.ShapeDtypeStruct((dests, count * BLOCK, LANE), BF),
        scratch_shapes=[
            pltpu.VMEM((2 * dests * MAIN, tokens), BF),
            pltpu.VMEM((2 * dests * FOLD, FOLD * tokens), BF),
        ],
        compiler_params=PARAMS,
        cost_estimate=pl.CostEstimate(
            flops=count * 2 * 1088 * 128 * WIDE, bytes_accessed=count * 3 << 20, transcendentals=0
        ),
        name="dispatch",
    )(ids, gates, grad, *after)


def natural(order, sources):
    main = sources * MAIN
    return jnp.where(order < main, (order // MAIN) * (MAIN + 1) + order % MAIN, (order - main) * (MAIN + 1) + MAIN)


def arrange_kernel(sources, gate_ref, up_ref, hidden_ref, gate_out_ref, up_out_ref):
    gate = gate_ref[0].astype(F32)
    slots = gate.shape[0]
    hidden = (gate * jax.nn.sigmoid(gate) * up_ref[0].astype(F32)).astype(BF)
    place = natural(iota((slots, slots), 1), sources) == iota((slots, slots), 0)
    place = jnp.where(place, 1.0, 0.0).astype(BF)
    hidden_ref[0] = dot(hidden, place, ((0,), (0,))).astype(BF)
    place = natural(iota((slots, slots), 0), sources) == iota((slots, slots), 1)
    place = jnp.where(place, 1.0, 0.0).astype(BF)
    gate_out_ref[0] = dot(place, gate_ref[0]).astype(BF)
    up_out_ref[0] = dot(place, up_ref[0]).astype(BF)


def arrange(gate, up, sources):
    local, slots, units = gate.shape
    spec = pl.BlockSpec((1, slots, units), lambda e: (e, 0, 0))
    return pl.pallas_call(
        functools.partial(arrange_kernel, sources),
        grid=(local,),
        in_specs=[spec, spec],
        out_specs=[pl.BlockSpec((1, units, slots), lambda e: (e, 0, 0)), spec, spec],
        out_shape=[jax.ShapeDtypeStruct((local, units, slots), BF)] + [jax.ShapeDtypeStruct(gate.shape, BF)] * 2,
        compiler_params=PARAMS,
        cost_estimate=pl.CostEstimate(flops=12 * slots * slots * units, bytes_accessed=9 << 20, transcendentals=0),
        name="arrange",
    )(gate, up)


def expert_rows(rows_ref, expert, out_ref):
    sources = rows_ref.shape[0]
    main = sources * MAIN
    for k in range(FOLD):
        at = (2 * k + expert) * MAIN
        out_ref[:main, k * LANE : (k + 1) * LANE] = rows_ref[:, at : at + MAIN, :].reshape(main, LANE)
    at = 2 * MAIN * FOLD
    folded = rows_ref[:, at : at + 2 * FOLD, :].reshape(sources * 2 * FOLD, LANE)
    row = iota((FOLD * sources, sources * 2 * FOLD), 0)
    column = iota((FOLD * sources, sources * 2 * FOLD), 1)
    pick = column == (row % sources) * 2 * FOLD + expert * FOLD + row // sources
    last = dot(jnp.where(pick, 1.0, 0.0).astype(BF), folded).astype(BF)
    for k in range(FOLD):
        out_ref[main:, k * LANE : (k + 1) * LANE] = last[k * sources : (k + 1) * sources]


def down_kernel(place_ref, rows_ref, hidden_ref, slots_ref, rest_ref, first_ref):
    e = pl.program_id(1)
    groups = rest_ref.shape[0]
    units = hidden_ref.shape[1] // groups
    for local in range(2):

        @pl.when(e == local)
        def _():
            expert_rows(rows_ref, local, slots_ref.at[0])

    for n in range(WIDE // 256):
        columns = slice(n * 256, (n + 1) * 256)
        total = dot(hidden_ref[0], slots_ref[0, :, columns]).astype(BF)
        for c in range(groups):
            turn = lax.rem(place_ref[1] * (place_ref[0] - c) - 1 + 2 * groups, groups)
            rest_ref[turn, :, columns] = total[c * units : (c + 1) * units]
    first_ref[...] = rest_ref[0]


def partial_down(place, arrived, hidden, groups, at, count):
    sources, _, _ = arrived.shape
    _, units, slots = hidden.shape
    rows = units // groups
    return pl.pallas_call(
        down_kernel,
        grid=(count, 2),
        in_specs=[
            pl.BlockSpec(memory_space=pltpu.SMEM),
            pl.BlockSpec((sources, BLOCK, LANE), lambda q, e: (0, at + q, 0)),
            pl.BlockSpec((1, units, slots), lambda q, e: (e, 0, 0)),
        ],
        out_specs=[
            pl.BlockSpec((1, slots, WIDE), lambda q, e: (e, 0, q)),
            pl.BlockSpec((groups, rows, WIDE), lambda q, e: (0, e, q)),
            pl.BlockSpec((rows, WIDE), lambda q, e: (e, q)),
        ],
        out_shape=[
            jax.ShapeDtypeStruct((2, slots, count * WIDE), BF),
            jax.ShapeDtypeStruct((groups, 2 * rows, count * WIDE), BF),
            jax.ShapeDtypeStruct((2 * rows, count * WIDE), BF),
        ],
        compiler_params=PARAMS,
        cost_estimate=pl.CostEstimate(
            flops=count * 4 * slots * units * WIDE, bytes_accessed=count * 9 << 20, transcendentals=0
        ),
        name="partial_down",
    )(place, arrived, hidden)


def hidden_grad_kernel(count, *refs):
    weight_ref, total_ref = refs[-2:]
    step = pl.program_id(0)
    groups, _, units, width = weight_ref.shape
    steps = 2 * WIDE // width
    slots_refs = refs[1 : 1 + count]

    @pl.when(step == 0)
    def _():
        total_ref[...] = refs[-3][...] if len(refs) == count + 4 else jnp.zeros_like(total_ref)

    for k, slots_ref in enumerate(slots_refs):

        @pl.when(step // (steps // count) == k)
        def _():
            weight = weight_ref[:, 0].reshape(groups * units, width)
            for n in range(0, groups * units, 256):
                total_ref[:, n : n + 256] += dot(slots_ref[0], weight[n : n + 256], ((1,), (1,)))


def hidden_grad(after, rows, weights, half, expert, before=()):
    groups, _, units, _ = weights.shape
    slots = rows[0].shape[1]
    width = WIDE // 2
    count = len(rows)
    each = 2 * WIDE // width // count
    whole = pl.BlockSpec((slots, groups * units), lambda k: (0, 0))
    specs = [
        pl.BlockSpec((1, slots, width), lambda k, j=j: (expert, 0, jnp.clip(k - j * each, 0, each - 1)))
        for j in range(count)
    ]
    return pl.pallas_call(
        functools.partial(hidden_grad_kernel, count),
        grid=(each * count,),
        in_specs=[pl.BlockSpec(memory_space=pltpu.SMEM)]
        + specs
        + [whole] * len(before)
        + [pl.BlockSpec((groups, 1, units, width), lambda k: (0, expert, 0, half * each * count + k))],
        out_specs=whole,
        out_shape=jax.ShapeDtypeStruct((slots, groups * units), F32),
        compiler_params=PARAMS,
        cost_estimate=pl.CostEstimate(
            flops=4 * slots * groups * units * WIDE, bytes_accessed=9 << 20, transcendentals=0
        ),
        name="hidden_grad",
    )(after, *rows, *before, weights)


def gate_grads_kernel(sources, after_ref, total_ref, gate_ref, up_ref, *refs):
    grad_gate_ref, grad_up_ref = refs[-2:]
    slots, _ = total_ref.shape
    back = natural(iota((slots, slots), 1), sources) == iota((slots, slots), 0)
    back = jnp.where(back, 1.0, 0.0).astype(BF)
    gate = gate_ref[0].astype(F32)
    up = up_ref[0].astype(F32)
    logistic = jax.nn.sigmoid(gate)
    grad = total_ref[...]
    grad_gate = (grad * up * logistic * (1.0 + gate * (1.0 - logistic))).astype(BF)
    grad_up = (grad * (gate * logistic)).astype(BF)
    grad_gate_ref[0] = dot(back, grad_gate).astype(BF)
    grad_up_ref[0] = dot(back, grad_up).astype(BF)


def gate_grads(after, total, gate, up, sources, expert, done=()):
    one = pl.BlockSpec((1,) + gate.shape[1:], lambda i: (expert, 0, 0))
    return pl.pallas_call(
        functools.partial(gate_grads_kernel, sources),
        grid=(1,),
        in_specs=[
            pl.BlockSpec(memory_space=pltpu.SMEM),
            pl.BlockSpec(total.shape, lambda i: (0, 0)),
            one,
            one,
        ]
        + [pl.BlockSpec(memory_space=pl.ANY)] * len(done),
        out_specs=[one, one],
        out_shape=[jax.ShapeDtypeStruct(gate.shape, BF)] * 2,
        input_output_aliases={4 + k: k for k in range(len(done))},
        compiler_params=PARAMS,
        cost_estimate=pl.CostEstimate(flops=4 * 544 * 544 * 768, bytes_accessed=5 << 20, transcendentals=0),
        name="gate_grads",
    )(after, total, gate, up, *done)


def final_kernel(after_ref, own_ref, arrived_ref, *refs):
    out_ref = refs[-1]
    units, _, _ = out_ref.shape
    value = arrived_ref[...].astype(F32) + own_ref[0].astype(F32)
    for e in range(2):
        out_ref[:, e, :] = value[e * units : (e + 1) * units]


def final(after, arrived, rest, shape, at, done=()):
    groups, rows, width = rest.shape
    return pl.pallas_call(
        final_kernel,
        grid=(width // WIDE,),
        in_specs=[
            pl.BlockSpec(memory_space=pltpu.SMEM),
            pl.BlockSpec((1, rows, WIDE), lambda i: (groups - 1, 0, i)),
            pl.BlockSpec((rows, WIDE), lambda i: (0, i)),
        ]
        + [pl.BlockSpec(memory_space=pl.ANY)] * len(done),
        out_specs=pl.BlockSpec((shape[0], 2, WIDE), lambda i: (0, 0, at + i)),
        out_shape=jax.ShapeDtypeStruct(shape, F32),
        input_output_aliases={3 + k: k for k in range(len(done))},
        compiler_params=PARAMS,
        cost_estimate=pl.CostEstimate(flops=rows * width, bytes_accessed=3 << 20, transcendentals=0),
        name="final",
    )(after, rest, arrived, *done)


class Clock:
    def __init__(self, value):
        self.value = value

    def __call__(self, value):
        value, self.value = lax.optimization_barrier((value, self.value))
        return value


class Ring:
    def __init__(self, clock, rest, blocks):
        self.clock, self.rest, self.turn = clock, rest, 0
        groups, members = lax.axis_size("dp"), lax.axis_size("expert")
        self.pairs = [
            (g * members + j, (g + 1 - 2 * (j % 2)) % groups * members + j)
            for g in range(groups)
            for j in range(members)
        ]
        self.send(blocks)

    def send(self, blocks):
        self.got = lax.ppermute(blocks, ("dp", "expert"), self.pairs)

    def step(self):
        self.turn += 1
        self.send(self.clock(self.clock(self.got) + self.rest[self.turn]))


def on_device(grad_out, expert_ids, gate_weights, saved_gate, saved_up, down_weight):
    sources = lax.axis_size("expert")
    groups = lax.axis_size("dp")
    units, local, width = down_weight.shape
    place = jnp.stack([lax.axis_index("dp"), 1 - 2 * (lax.axis_index("expert") % 2)]).astype(jnp.int32)
    clock = Clock(place)

    def exchange(rows):
        return lax.all_to_all(rows, "expert", split_axis=0, concat_axis=0, tiled=True)

    weights = lax.all_gather(jnp.transpose(down_weight, (1, 0, 2)), "dp", axis=0, tiled=False)
    first = exchange(dispatch(expert_ids, gate_weights, grad_out, sources, 0, 2))
    hidden, gate, up = arrange(saved_gate, saved_up, sources)
    second = exchange(dispatch(expert_ids, gate_weights, grad_out, sources, 2, 2, (hidden,)))

    slots, rings, total = [], [], [(), ()]
    for arrived in (first, second):
        rows, rest, sent = partial_down(place, clock(arrived), hidden, groups, 0, 2)
        slots.append(rows)
        rings.append(Ring(clock, rest, clock(sent)))
        if len(rings) == 1:
            rings[0].step()

    def hidden_piece(half, e):
        piece = hidden_grad(clock.value, [slots[half]], weights, half, e, total[e])
        total[e] = (clock(piece),)

    def gate_piece(e, done):
        return clock(gate_grads(clock.value, total[e][0], gate, up, sources, e, done))

    grads = ()
    for turn in range(1, groups - 1):
        if rings[0].turn < groups - 2:
            rings[0].step()
        if turn in (1, 2, 4, 5):
            hidden_piece((turn - 1) % 3, turn // 3)
        else:
            grads = gate_piece(turn // 3 - 1, grads)
        rings[1].step()
    out_shape, grad_down = (units, local, width), ()
    for half in range(2):
        got = clock(rings[half].got)
        grad_down = (final(clock.value, got, rings[half].rest, out_shape, 2 * half, grad_down),)
    return (grads[0], grads[1], grad_down[0])


def solution(mesh):
    in_specs = (
        P(("dp", "expert"), None),
        P(("dp", "expert"), None),
        P(("dp", "expert"), None),
        P("expert", "dp", None),
        P("expert", "dp", None),
        P("dp", "expert", None),
    )
    out_specs = (P("expert", "dp", None), P("expert", "dp", None), P("dp", "expert", None))
    return jax.shard_map(
        on_device, mesh=mesh, in_specs=in_specs, out_specs=out_specs, check_vma=False
    )
```

```python
import functools

import jax
import jax.numpy as jnp
from jax import lax
from jax.experimental import pallas as pl
from jax.experimental.pallas import tpu as pltpu
from jax.sharding import PartitionSpec as P

BF = jnp.bfloat16
F32 = jnp.float32
LANE = 128
MAIN = 16
FOLD = 8
WIDE = FOLD * LANE
BLOCK = 2 * MAIN * FOLD + 2 * FOLD
PARAMS = pltpu.CompilerParams(vmem_limit_bytes=56 * 1024 * 1024)


def dot(a, b, dims=((1,), (0,))):
    return lax.dot_general(a, b, (dims, ((), ())), preferred_element_type=F32)


def iota(shape, dim):
    return lax.broadcasted_iota(jnp.int32, shape, dim)


def dispatch_kernel(ids_ref, gates_ref, grad_ref, *refs):
    out_ref, main_ref, tail_ref = refs[-3:]
    top, tokens = ids_ref.shape
    dests = out_ref.shape[0]
    experts = 2 * dests

    @pl.when(pl.program_id(0) == 0)
    def _():
        expert = iota((experts, tokens), 0)
        member = jnp.zeros((experts, tokens), F32)
        gate = jnp.zeros((experts, tokens), F32)
        gates = gates_ref[...].astype(F32)
        for k in range(top):
            hit = ids_ref[k : k + 1, :] == expert
            member = jnp.where(hit, 1.0, member)
            gate = jnp.where(hit, gates[k : k + 1, :], gate)
        earlier = jnp.where(iota((tokens, tokens), 0) < iota((tokens, tokens), 1), 1.0, 0.0)
        rank = dot(member.astype(BF), earlier.astype(BF))
        rank = jnp.where(member > 0.0, rank, -1.0)
        slots = iota((experts, MAIN, tokens), 1).astype(F32)
        chosen = jnp.where(rank[:, None, :] == slots, gate[:, None, :], 0.0)
        main_ref[...] = chosen.reshape(experts * MAIN, tokens).astype(BF)
        last = jnp.where(rank == float(MAIN), gate, 0.0)
        last = jnp.broadcast_to(last[:, None, :], (experts, FOLD, tokens)).reshape(experts * FOLD, tokens)
        rows = iota((experts * FOLD, tokens), 0) % FOLD
        for k in range(FOLD):
            tail_ref[:, k * tokens : (k + 1) * tokens] = jnp.where(rows == k, last, 0.0).astype(BF)

    for pair in range(FOLD // 2):
        rows = dot(main_ref[...], grad_ref[:, pair * 256 : (pair + 1) * 256]).astype(BF)
        for k in range(2):
            at = (2 * pair + k) * 2 * MAIN
            out_ref[:, at : at + 2 * MAIN, :] = rows[:, k * LANE : (k + 1) * LANE].reshape(dests, 2 * MAIN, LANE)
    stacked = jnp.concatenate([grad_ref[:, k * LANE : (k + 1) * LANE] for k in range(FOLD)], axis=0)
    rows = dot(tail_ref[...], stacked).astype(BF)
    out_ref[:, 2 * MAIN * FOLD :, :] = rows.reshape(dests, 2 * FOLD, LANE)


def dispatch(ids, gates, grad, dests, first, count, after=()):
    tokens, _ = grad.shape
    ids, gates = jnp.transpose(ids), jnp.transpose(gates)
    return pl.pallas_call(
        dispatch_kernel,
        grid=(count,),
        in_specs=[
            pl.BlockSpec(ids.shape, lambda i: (0, 0)),
            pl.BlockSpec(gates.shape, lambda i: (0, 0)),
            pl.BlockSpec((tokens, WIDE), lambda i: (0, first + i)),
        ]
        + [pl.BlockSpec(memory_space=pl.ANY)] * len(after),
        out_specs=pl.BlockSpec((dests, BLOCK, LANE), lambda i: (0, i, 0)),
        out_shape=jax.ShapeDtypeStruct((dests, count * BLOCK, LANE), BF),
        scratch_shapes=[
            pltpu.VMEM((2 * dests * MAIN, tokens), BF),
            pltpu.VMEM((2 * dests * FOLD, FOLD * tokens), BF),
        ],
        compiler_params=PARAMS,
        cost_estimate=pl.CostEstimate(
            flops=count * 2 * 1088 * 128 * WIDE, bytes_accessed=count * 3 << 20, transcendentals=0
        ),
        name="dispatch",
    )(ids, gates, grad, *after)


def natural(order, sources):
    main = sources * MAIN
    return jnp.where(order < main, (order // MAIN) * (MAIN + 1) + order % MAIN, (order - main) * (MAIN + 1) + MAIN)


def arrange_kernel(sources, gate_ref, up_ref, hidden_ref, gate_out_ref, up_out_ref):
    gate = gate_ref[0].astype(F32)
    slots = gate.shape[0]
    hidden = (gate * jax.nn.sigmoid(gate) * up_ref[0].astype(F32)).astype(BF)
    place = natural(iota((slots, slots), 1), sources) == iota((slots, slots), 0)
    place = jnp.where(place, 1.0, 0.0).astype(BF)
    hidden_ref[0] = dot(hidden, place, ((0,), (0,))).astype(BF)
    place = natural(iota((slots, slots), 0), sources) == iota((slots, slots), 1)
    place = jnp.where(place, 1.0, 0.0).astype(BF)
    gate_out_ref[0] = dot(place, gate_ref[0]).astype(BF)
    up_out_ref[0] = dot(place, up_ref[0]).astype(BF)


def arrange(gate, up, sources):
    local, slots, units = gate.shape
    spec = pl.BlockSpec((1, slots, units), lambda e: (e, 0, 0))
    return pl.pallas_call(
        functools.partial(arrange_kernel, sources),
        grid=(local,),
        in_specs=[spec, spec],
        out_specs=[pl.BlockSpec((1, units, slots), lambda e: (e, 0, 0)), spec, spec],
        out_shape=[jax.ShapeDtypeStruct((local, units, slots), BF)] + [jax.ShapeDtypeStruct(gate.shape, BF)] * 2,
        compiler_params=PARAMS,
        cost_estimate=pl.CostEstimate(flops=12 * slots * slots * units, bytes_accessed=9 << 20, transcendentals=0),
        name="arrange",
    )(gate, up)


def expert_rows(rows_ref, expert, out_ref):
    sources = rows_ref.shape[0]
    main = sources * MAIN
    for k in range(FOLD):
        at = (2 * k + expert) * MAIN
        out_ref[:main, k * LANE : (k + 1) * LANE] = rows_ref[:, at : at + MAIN, :].reshape(main, LANE)
    at = 2 * MAIN * FOLD
    folded = rows_ref[:, at : at + 2 * FOLD, :].reshape(sources * 2 * FOLD, LANE)
    row = iota((FOLD * sources, sources * 2 * FOLD), 0)
    column = iota((FOLD * sources, sources * 2 * FOLD), 1)
    pick = column == (row % sources) * 2 * FOLD + expert * FOLD + row // sources
    last = dot(jnp.where(pick, 1.0, 0.0).astype(BF), folded).astype(BF)
    for k in range(FOLD):
        out_ref[main:, k * LANE : (k + 1) * LANE] = last[k * sources : (k + 1) * sources]


def down_kernel(place_ref, rows_ref, hidden_ref, slots_ref, rest_ref, first_ref):
    e = pl.program_id(1)
    groups = rest_ref.shape[0]
    units = hidden_ref.shape[1] // groups
    for local in range(2):

        @pl.when(e == local)
        def _():
            expert_rows(rows_ref, local, slots_ref.at[0])

    for n in range(WIDE // 256):
        columns = slice(n * 256, (n + 1) * 256)
        total = dot(hidden_ref[0], slots_ref[0, :, columns]).astype(BF)
        for c in range(groups):
            turn = lax.rem(place_ref[1] * (place_ref[0] - c) - 1 + 2 * groups, groups)
            rest_ref[turn, :, columns] = total[c * units : (c + 1) * units]
    first_ref[...] = rest_ref[0]


def partial_down(place, arrived, hidden, groups, at, count):
    sources, _, _ = arrived.shape
    _, units, slots = hidden.shape
    rows = units // groups
    return pl.pallas_call(
        down_kernel,
        grid=(count, 2),
        in_specs=[
            pl.BlockSpec(memory_space=pltpu.SMEM),
            pl.BlockSpec((sources, BLOCK, LANE), lambda q, e: (0, at + q, 0)),
            pl.BlockSpec((1, units, slots), lambda q, e: (e, 0, 0)),
        ],
        out_specs=[
            pl.BlockSpec((1, slots, WIDE), lambda q, e: (e, 0, q)),
            pl.BlockSpec((groups, rows, WIDE), lambda q, e: (0, e, q)),
            pl.BlockSpec((rows, WIDE), lambda q, e: (e, q)),
        ],
        out_shape=[
            jax.ShapeDtypeStruct((2, slots, count * WIDE), BF),
            jax.ShapeDtypeStruct((groups, 2 * rows, count * WIDE), BF),
            jax.ShapeDtypeStruct((2 * rows, count * WIDE), BF),
        ],
        compiler_params=PARAMS,
        cost_estimate=pl.CostEstimate(
            flops=count * 4 * slots * units * WIDE, bytes_accessed=count * 9 << 20, transcendentals=0
        ),
        name="partial_down",
    )(place, arrived, hidden)


def hidden_grad_kernel(count, *refs):
    weight_ref, total_ref = refs[-2:]
    step = pl.program_id(0)
    groups, _, units, width = weight_ref.shape
    steps = 2 * WIDE // width
    slots_refs = refs[1 : 1 + count]

    @pl.when(step == 0)
    def _():
        total_ref[...] = refs[-3][...] if len(refs) == count + 4 else jnp.zeros_like(total_ref)

    for k, slots_ref in enumerate(slots_refs):

        @pl.when(step // (steps // count) == k)
        def _():
            weight = weight_ref[:, 0].reshape(groups * units, width)
            for n in range(0, groups * units, 256):
                total_ref[:, n : n + 256] += dot(slots_ref[0], weight[n : n + 256], ((1,), (1,)))


def hidden_grad(after, rows, weights, half, expert, before=()):
    groups, _, units, _ = weights.shape
    slots = rows[0].shape[1]
    width = WIDE // 2
    count = len(rows)
    each = 2 * WIDE // width // count
    whole = pl.BlockSpec((slots, groups * units), lambda k: (0, 0))
    specs = [
        pl.BlockSpec((1, slots, width), lambda k, j=j: (expert, 0, jnp.clip(k - j * each, 0, each - 1)))
        for j in range(count)
    ]
    return pl.pallas_call(
        functools.partial(hidden_grad_kernel, count),
        grid=(each * count,),
        in_specs=[pl.BlockSpec(memory_space=pltpu.SMEM)]
        + specs
        + [whole] * len(before)
        + [pl.BlockSpec((groups, 1, units, width), lambda k: (0, expert, 0, half * each * count + k))],
        out_specs=whole,
        out_shape=jax.ShapeDtypeStruct((slots, groups * units), F32),
        compiler_params=PARAMS,
        cost_estimate=pl.CostEstimate(
            flops=4 * slots * groups * units * WIDE, bytes_accessed=9 << 20, transcendentals=0
        ),
        name="hidden_grad",
    )(after, *rows, *before, weights)


def gate_grads_kernel(sources, after_ref, total_ref, gate_ref, up_ref, *refs):
    grad_gate_ref, grad_up_ref = refs[-2:]
    slots, _ = total_ref.shape
    back = natural(iota((slots, slots), 1), sources) == iota((slots, slots), 0)
    back = jnp.where(back, 1.0, 0.0).astype(BF)
    gate = gate_ref[0].astype(F32)
    up = up_ref[0].astype(F32)
    logistic = jax.nn.sigmoid(gate)
    grad = total_ref[...]
    grad_gate = (grad * up * logistic * (1.0 + gate * (1.0 - logistic))).astype(BF)
    grad_up = (grad * (gate * logistic)).astype(BF)
    grad_gate_ref[0] = dot(back, grad_gate).astype(BF)
    grad_up_ref[0] = dot(back, grad_up).astype(BF)


def gate_grads(after, total, gate, up, sources, expert, done=()):
    one = pl.BlockSpec((1,) + gate.shape[1:], lambda i: (expert, 0, 0))
    return pl.pallas_call(
        functools.partial(gate_grads_kernel, sources),
        grid=(1,),
        in_specs=[
            pl.BlockSpec(memory_space=pltpu.SMEM),
            pl.BlockSpec(total.shape, lambda i: (0, 0)),
            one,
            one,
        ]
        + [pl.BlockSpec(memory_space=pl.ANY)] * len(done),
        out_specs=[one, one],
        out_shape=[jax.ShapeDtypeStruct(gate.shape, BF)] * 2,
        input_output_aliases={4 + k: k for k in range(len(done))},
        compiler_params=PARAMS,
        cost_estimate=pl.CostEstimate(flops=4 * 544 * 544 * 768, bytes_accessed=5 << 20, transcendentals=0),
        name="gate_grads",
    )(after, total, gate, up, *done)


def final_kernel(after_ref, own_ref, arrived_ref, *refs):
    out_ref = refs[-1]
    units, _, _ = out_ref.shape
    value = arrived_ref[...].astype(F32) + own_ref[0].astype(F32)
    for e in range(2):
        out_ref[:, e, :] = value[e * units : (e + 1) * units]


def final(after, arrived, rest, shape, at, done=()):
    groups, rows, width = rest.shape
    return pl.pallas_call(
        final_kernel,
        grid=(1,),
        in_specs=[
            pl.BlockSpec(memory_space=pltpu.SMEM),
            pl.BlockSpec((1, rows, width), lambda i: (groups - 1, 0, 0)),
            pl.BlockSpec((rows, width), lambda i: (0, 0)),
        ]
        + [pl.BlockSpec(memory_space=pl.ANY)] * len(done),
        out_specs=pl.BlockSpec((shape[0], 2, width), lambda i: (0, 0, at)),
        out_shape=jax.ShapeDtypeStruct(shape, F32),
        input_output_aliases={3 + k: k for k in range(len(done))},
        compiler_params=PARAMS,
        cost_estimate=pl.CostEstimate(flops=rows * width, bytes_accessed=3 << 20, transcendentals=0),
        name="final",
    )(after, rest, arrived, *done)


class Clock:
    def __init__(self, value):
        self.value = value

    def __call__(self, value):
        value, self.value = lax.optimization_barrier((value, self.value))
        return value


class Ring:
    def __init__(self, clock, rest, blocks):
        self.clock, self.rest, self.turn = clock, rest, 0
        groups, members = lax.axis_size("dp"), lax.axis_size("expert")
        self.pairs = [
            (g * members + j, (g + 1 - 2 * (j % 2)) % groups * members + j)
            for g in range(groups)
            for j in range(members)
        ]
        self.send(blocks)

    def send(self, blocks):
        self.got = lax.ppermute(blocks, ("dp", "expert"), self.pairs)

    def step(self):
        self.turn += 1
        self.send(self.clock(self.clock(self.got) + self.rest[self.turn]))


def on_device(grad_out, expert_ids, gate_weights, saved_gate, saved_up, down_weight):
    sources = lax.axis_size("expert")
    groups = lax.axis_size("dp")
    units, local, width = down_weight.shape
    place = jnp.stack([lax.axis_index("dp"), 1 - 2 * (lax.axis_index("expert") % 2)]).astype(jnp.int32)
    clock = Clock(place)

    def exchange(rows):
        return lax.all_to_all(rows, "expert", split_axis=0, concat_axis=0, tiled=True)

    weights = lax.all_gather(jnp.transpose(down_weight, (1, 0, 2)), "dp", axis=0, tiled=False)
    first = exchange(dispatch(expert_ids, gate_weights, grad_out, sources, 0, 2))
    hidden, gate, up = arrange(saved_gate, saved_up, sources)
    second = exchange(dispatch(expert_ids, gate_weights, grad_out, sources, 2, 2, (hidden,)))

    slots, rings, total = [], [], [(), ()]
    for arrived in (first, second):
        rows, rest, sent = partial_down(place, clock(arrived), hidden, groups, 0, 2)
        slots.append(rows)
        rings.append(Ring(clock, rest, clock(sent)))
        if len(rings) == 1:
            rings[0].step()

    def hidden_piece(half, e):
        piece = hidden_grad(clock.value, [slots[half]], weights, half, e, total[e])
        total[e] = (clock(piece),)

    def gate_piece(e, done):
        return clock(gate_grads(clock.value, total[e][0], gate, up, sources, e, done))

    grads = ()
    for turn in range(1, groups - 1):
        if rings[0].turn < groups - 2:
            rings[0].step()
        rings[1].step()
        if turn in (1, 2, 4, 5):
            hidden_piece((turn - 1) % 3, turn // 3)
        else:
            grads = gate_piece(turn // 3 - 1, grads)
    out_shape, grad_down = (units, local, width), ()
    for half in range(2):
        got = clock(rings[half].got)
        grad_down = (final(clock.value, got, rings[half].rest, out_shape, half, grad_down),)
    return (grads[0], grads[1], grad_down[0])


def solution(mesh):
    in_specs = (
        P(("dp", "expert"), None),
        P(("dp", "expert"), None),
        P(("dp", "expert"), None),
        P("expert", "dp", None),
        P("expert", "dp", None),
        P("dp", "expert", None),
    )
    out_specs = (P("expert", "dp", None), P("expert", "dp", None), P("dp", "expert", None))
    return jax.shard_map(
        on_device, mesh=mesh, in_specs=in_specs, out_specs=out_specs, check_vma=False
    )
```
